32 devices in a mesh: groups: 2 (over x), rows: 16 (over z, y, core).
Axes of the slice: x: 2, y: 2, z: 4, core: 2. Of those that a mesh axis runs over, the one named last changes fastest.
Arguments:
- features: bfloat16 [512, 256, 128], P('rows', 'groups'), parts along dimension 1, may hold values from -6 to 6
- weights: bfloat16 [1, 512, 8, 128, 128], P(None, 'rows'), may hold values from -0.25 to 0.25
- biases: float32 [1, 512, 128], P(None, 'rows'), may hold values from -3 to 3
- dest_dev: int32 [1, 512, 8], replicated, may hold values from 0 to 15, all different within a row; in each aligned block of 32 rows (0 to 31, 32 to 63, ..., all dimensions but the last counted through in order) at most 32 rows name the same one
- dest_local: int32 [1, 512, 8], replicated, may hold values from 0 to 31
Outputs:
- outputs: bfloat16 [512, 256, 128], P('rows', 'groups'), parts along dimension 1
The draws below stay inside these ranges and needn't reach their ends.
There are 2 independent parts, one for each index of `groups`. The reference program is written for one: setup_inputs(seed, part) draws one part's arguments, and reference() takes and returns one part's arrays. A program takes and returns all parts, laid end to end along the dimension named above; an argument that names none is the same for every part. Nothing has to cross between parts.
Inputs may be any that keep to these rules, and one draw needn't show every extreme that they name: `dest_dev`: the 8 entries of one input block name different owners; in one layer, the 32 input blocks of one owner name any one owner at most 32 times, and in some layers some owner is named exactly 32 times by one owner's blocks.
All inputs are finite; a program needn't handle non-finite values.
Results may differ from the reference program's by a relative error of at most 0.001.
Values sent between devices are 32-bit elements; how exact they have to be, the bound alone decides.
A program may use at most 320 MiB of HBM per device.

```python
import math
import jax
import jax.numpy as jnp
import numpy as np
from jax import lax

BS = 128
DEG = 8
LAYERS = 1
SAMPLES = 128
NBLK = 512
OWNERS = 16
OWN = 32
CAP = 32
N_ROWS = 16


def touch_ends(drawn, own_key, low, top_value):
    longest = drawn.shape.index(max(drawn.shape))
    spots = []
    for shift in (0, 1):
        where = [jax.random.randint(jax.random.fold_in(own_key, axis), (), 0, length) for axis, length in enumerate(drawn.shape)]
        where[longest] = (where[longest] + shift) % drawn.shape[longest]
        spots.append(tuple(where))
    return drawn.at[spots[0]].set(low).at[spots[1]].set(top_value)


def block_scale(own_key, shape, split, low, largest):
    factor_of = 1.0
    for dim, parts in split:
        draws = jax.random.uniform(jax.random.fold_in(jax.random.fold_in(own_key, 6), dim), (parts,), jnp.float32, low / len(split), largest / len(split))
        factor_of = factor_of * jnp.repeat(jnp.exp(draws), shape[dim] // parts).reshape((-1,) + (1,) * (len(shape) - 1 - dim))
    return factor_of


def assign_block(key, own, number, rows, number_of, top, limit, lean):
    order = jax.random.permutation(key, number_of)
    heavy_load, usual = portions_of(number_of, rows * top, limit, lean, True), portions_of(number_of, rows * top, limit, lean, False)
    places = jnp.arange(number_of)

    def named(lengths, turn):
        used = int((lengths > 0).sum())
        fixed = max(1, used // 4)
        moved = fixed + (places - fixed + turn * (used - fixed)) % max(1, number_of - fixed)
        return jnp.zeros((number_of,), jnp.int32).at[order[jnp.where(places < fixed, places, moved)]].set(jnp.asarray(lengths, jnp.int32))

    lengths = jnp.where(number % 4 == 0, named(heavy_load, number // 4), named(usual, number - number // 4 - 1))
    mixed = jax.random.permutation(jax.random.fold_in(own, 3), number_of)
    source_of, sink = mixed[0:number_of // 2 * 2:2], mixed[1:number_of // 2 * 2:2]
    slack = jnp.minimum(lengths[source_of] - 1, limit - lengths[sink]) // 2
    slack = jnp.where((source_of == order[0]) | (sink == order[0]) | (lengths[sink] == 0), 0, jnp.maximum(slack, 0))
    moved = jax.random.randint(jax.random.fold_in(own, 4), (number_of // 2,), 0, 1 << 20) % (slack + 1)
    lengths = lengths.at[source_of].add(-moved).at[sink].add(moved)
    members = jnp.searchsorted(jnp.cumsum(lengths), jnp.arange(rows * top), side="right").astype(jnp.int32)
    listing = members.reshape(top, rows).T
    listing = listing[jax.random.permutation(jax.random.fold_in(own, 1), rows)]
    turn = jax.random.randint(jax.random.fold_in(own, 2), (rows, 1), 0, top)
    return jnp.take_along_axis(listing, (jnp.arange(top)[None, :] + turn) % top, axis=1)


def portions_of(number_of, total, most, lean, full):
    weights = [(1 << 20) // math.isqrt(rank ** lean) + 1 for rank in range(1, number_of + 1)]
    largest = most if full else min(most, max(-(-total // number_of), total * weights[0] // sum(weights)))
    least = 1 if total - largest >= number_of - 1 else 0
    counts, rest = [largest] + [least] * (number_of - 1), total - largest - least * (number_of - 1)
    while rest > 0:
        movable = [i for i in range(1, number_of) if counts[i] < largest] or [i for i in range(1, number_of) if counts[i] < most]
        whole, left = sum([weights[i] for i in movable]), rest
        for i in movable:
            extra = min(most - counts[i], max(1, left * weights[i] // whole), rest)
            counts[i] = counts[i] + extra
            rest = rest - extra
    return np.array(counts)


def gaussian(rng, dims, spread, bound, pieces=(), dtype=jnp.bfloat16):
    drawn = spread * jax.random.normal(rng, dims, jnp.float32)
    if pieces:
        drawn = drawn * block_scale(rng, dims, pieces, -0.22, 0.18)
    return jnp.clip(drawn, -bound, bound).astype(dtype)


def setup_inputs(seed: int = 0, part: int = 0) -> dict:
    splits = jax.random.split(jax.random.key(seed), 6)
    part_splits = jax.random.split(jax.random.fold_in(splits[5], part), 6)
    features = gaussian(part_splits[0], (NBLK, SAMPLES, BS), 1.0, 6.0, ((0, 16),))
    weights = gaussian(splits[1], (LAYERS, NBLK, DEG, BS, BS), (BS * DEG // 2) ** -0.5, 0.25, ((1, 16),))
    biases = gaussian(splits[2], (LAYERS, NBLK, BS), 0.5, 3.0, ((1, 16),), jnp.float32)
    dest_dev_keys = jax.random.split(jax.random.fold_in(splits[3], 1), LAYERS * NBLK // OWN)
    dest_dev_turns = jax.random.permutation(jax.random.fold_in(splits[3], 3), LAYERS * NBLK // OWN)
    dest_dev = jax.vmap(lambda own, number: assign_block(jax.random.fold_in(splits[3], 2), own, number, OWN, OWNERS, DEG, CAP, 2))(dest_dev_keys, dest_dev_turns).reshape((LAYERS, NBLK, DEG))
    dest_local = touch_ends(jax.random.randint(splits[4], (LAYERS, NBLK, DEG), 0, OWN), jax.random.fold_in(splits[4], 1), 0, OWN - 1).astype(jnp.int32)
    return {"features": features, "weights": weights, "biases": biases, "dest_dev": dest_dev, "dest_local": dest_local}


def reference(features, weights, biases, dest_dev, dest_local):
    activity = features
    for layer_index in range(LAYERS):
        position = (dest_dev[layer_index] * OWN + dest_local[layer_index]).astype(jnp.int32)
        position = position.reshape(N_ROWS, OWN * DEG)
        inputs_grouped = activity.reshape(N_ROWS, OWN, SAMPLES, BS)
        weight_grouped = weights[layer_index].reshape(N_ROWS, OWN, DEG, BS, BS)

        def accumulate(running, slab_group):
            block_in, block_weight, block_pos = slab_group
            products = jnp.einsum('osi,odij->odsj', block_in.astype(jnp.float32), block_weight.astype(jnp.float32))
            products = products.reshape(OWN * DEG, SAMPLES, BS)
            return running + jax.ops.segment_sum(products, block_pos, num_segments=NBLK), None

        start_sum = jnp.zeros((NBLK, SAMPLES, BS), jnp.float32)
        running, _ = lax.scan(accumulate, start_sum, (inputs_grouped, weight_grouped, position))
        activity = jax.nn.relu(running + biases[layer_index][:, None, :]).astype(jnp.bfloat16)
    return activity
```

```python
import functools

import jax
import jax.numpy as jnp
from jax import lax
from jax.experimental import pallas as pl
from jax.experimental.pallas import tpu as pltpu
from jax.sharding import PartitionSpec as P

MIB = 1024 * 1024


def partial_kernel(pos_ref, feat_ref, weight_ref, out_ref, acc, sem):
    step = pl.program_id(0)
    per_step, degree = weight_ref.shape[:2]
    owners, owned = acc.shape[:2]

    @pl.when(step == 0)
    def _():
        @pl.loop(0, owners)
        def _(o):
            @pl.loop(0, owned)
            def _(b):
                acc[o, b] = jnp.zeros(acc.shape[2:], acc.dtype)

    @pl.loop(0, per_step)
    def _(i):
        block = feat_ref[i]
        products = [
            jnp.dot(block, weight_ref[i, k], preferred_element_type=jnp.float32)
            for k in range(degree)
        ]
        base = (step * per_step + i) * degree
        for k in range(degree):
            position = pos_ref[base + k]
            acc[position // owned, position % owned] += products[k]

    @pl.when(step == pl.num_programs(0) - 1)
    def _():
        copy = pltpu.make_async_copy(acc, out_ref, sem)
        copy.start()
        copy.wait()


def local_partials(position, features, weights, owners, owned):
    count, samples, width = features.shape
    degree = weights.shape[1]
    per_step = min(4, count)
    return pl.pallas_call(
        partial_kernel,
        out_shape=jax.ShapeDtypeStruct((owners, owned, samples, width), jnp.float32),
        grid_spec=pltpu.PrefetchScalarGridSpec(
            num_scalar_prefetch=1,
            grid=(count // per_step,),
            in_specs=[
                pl.BlockSpec((per_step, samples, width), lambda s, pos: (s, 0, 0)),
                pl.BlockSpec((per_step, degree, width, width), lambda s, pos: (s, 0, 0, 0)),
            ],
            out_specs=pl.BlockSpec(memory_space=pl.ANY),
            scratch_shapes=[
                pltpu.VMEM((owners, owned, samples, width), jnp.float32),
                pltpu.SemaphoreType.DMA,
            ],
        ),
        compiler_params=pltpu.CompilerParams(
            dimension_semantics=("arbitrary",), vmem_limit_bytes=48 * MIB
        ),
    )(position, features, weights)


def farthest_first(z, nz):
    near = jnp.minimum(z, nz - 1 - z)
    far = nz - 1 - near
    sign = jnp.where(2 * z < nz, 1, -1)
    places = []
    for t in range(nz):
        u = t - (far - near)
        alone = z + sign * (far - t)
        paired = jnp.where(u % 2 == 0, z + sign * (near - u // 2), z - sign * (near - u // 2))
        places.append(jnp.where(u < 0, alone, paired))
    return places


def scatter_kernel(nz, ny, p_ref, bias_ref, out_ref, held, own, from_y, from_low, from_high,
                   own_sem, c_send, c_recv, y_send, y_recv, up_send, up_recv, down_send, down_recv):
    rank = lax.axis_index("rows")
    c = rank % 2
    y = (rank // 2) % ny
    z = rank // (2 * ny)
    owned = out_ref.shape[0]

    def row(z_at, y_at, c_at):
        return (z_at * ny + y_at) * 2 + c_at

    def remote(src, dst, send, recv, target):
        return pltpu.make_async_remote_copy(
            src_ref=src, dst_ref=dst, send_sem=send, recv_sem=recv,
            device_id={"rows": target}, device_id_type=pl.DeviceIdType.MESH,
        )

    sibling = row(z, y, 1 - c)
    peer = row(z, ny - 1 - y, c)
    above = row(z + 1, y, c)
    below = row(z - 1, y, c)
    has_above, has_below = z < nz - 1, z > 0

    barrier = pltpu.get_barrier_semaphore()

    def greet(target):
        pl.semaphore_signal(
            barrier, inc=1, device_id={"rows": target}, device_id_type=pl.DeviceIdType.MESH
        )

    greet(sibling)
    if ny > 1:
        greet(peer)
    pl.when(has_above)(lambda: greet(above))
    pl.when(has_below)(lambda: greet(below))
    pl.semaphore_wait(barrier, ny + jnp.where(has_above, 1, 0) + jnp.where(has_below, 1, 0))

    def add(dst, srcs):
        @pl.loop(0, owned)
        def _(b):
            total = dst[b]
            for src in srcs:
                total = total + src[b]
            dst[b] = total

    order = farthest_first(z, nz)

    def y_of(h):
        return y if h == ny - 1 else ny - 1 - y

    pieces = [(h, place) for place in order for h in range(ny)]

    def to_sibling(h, place):
        return remote(p_ref.at[row(place, y_of(h), 1 - c)], held.at[h, place],
                      c_send.at[h, place], c_recv.at[h, place], sibling)

    def load(n):
        h, place = pieces[n]
        return pltpu.make_async_copy(
            p_ref.at[row(place, y_of(h), c)], own.at[n % 2], own_sem.at[n % 2]
        )

    def to_peer(place):
        return remote(held.at[0, place], from_y.at[place], y_send.at[place], y_recv.at[place], peer)

    def to_above(place):
        return remote(held.at[ny - 1, place], from_low.at[place - 1],
                      up_send.at[place - 1], up_recv.at[place - 1], above)

    def to_below(place):
        return remote(held.at[ny - 1, place], from_high.at[place],
                      down_send.at[place], down_recv.at[place], below)

    load(0).start()
    for h, place in pieces:
        to_sibling(h, place).start()
    for n, (h, place) in enumerate(pieces):
        if n + 1 < len(pieces):
            load(n + 1).start()
        load(n).wait()
        to_sibling(h, place).wait_recv()
        add(held.at[h, place], [own.at[n % 2]])
        if h < ny - 1:
            to_peer(place).start()

    for t, place in enumerate(order[:-1]):
        if ny > 1:
            to_peer(place).wait_recv()
            add(held.at[ny - 1, place], [from_y.at[place]])

        @pl.when(place > z)
        def _():
            @pl.when(has_below)
            def _():
                to_above(place).wait_recv()
                add(held.at[ny - 1, place], [from_low.at[place - 1]])
            to_above(place).start()

        @pl.when(place < z)
        def _():
            @pl.when(has_above)
            def _():
                to_below(place).wait_recv()
                add(held.at[ny - 1, place], [from_high.at[place]])
            to_below(place).start()

    if ny > 1:
        to_peer(z).wait_recv()
        add(held.at[ny - 1, z], [from_y.at[z]])

    @pl.when(has_below)
    def _():
        to_above(z).wait_recv()
        add(held.at[ny - 1, z], [from_low.at[z - 1]])

    @pl.when(has_above)
    def _():
        to_below(z).wait_recv()
        add(held.at[ny - 1, z], [from_high.at[z]])

    @pl.loop(0, owned)
    def _(b):
        total = held[ny - 1, z, b] + bias_ref[b]
        out_ref[b] = jnp.maximum(total, 0.0).astype(out_ref.dtype)

    for h, place in pieces:
        to_sibling(h, place).wait_send()
    for place in order:
        if ny > 1:
            to_peer(place).wait_send()
        pl.when(place > z)(lambda place=place: to_above(place).wait_send())
        pl.when(place < z)(lambda place=place: to_below(place).wait_send())


def scatter_sum(partials, bias, nz, ny):
    owners, owned, samples, width = partials.shape
    chunk = (owned, samples, width)
    dma = pltpu.SemaphoreType.DMA
    vmem = pl.BlockSpec(memory_space=pltpu.VMEM)
    return pl.pallas_call(
        functools.partial(scatter_kernel, nz, ny),
        out_shape=jax.ShapeDtypeStruct(chunk, jnp.bfloat16),
        in_specs=[pl.BlockSpec(memory_space=pl.ANY), vmem],
        out_specs=vmem,
        scratch_shapes=[
            pltpu.VMEM((ny, nz) + chunk, jnp.float32),
            pltpu.VMEM((2,) + chunk, jnp.float32),
            pltpu.VMEM((nz if ny > 1 else 1,) + chunk, jnp.float32),
            pltpu.VMEM((nz - 1,) + chunk, jnp.float32),
            pltpu.VMEM((nz - 1,) + chunk, jnp.float32),
            dma((2,)),
            dma((ny, nz)), dma((ny, nz)),
            dma((nz,)), dma((nz,)),
            dma((nz,)), dma((nz,)),
            dma((nz,)), dma((nz,)),
        ],
        compiler_params=pltpu.CompilerParams(
            collective_id=0, has_side_effects=True, vmem_limit_bytes=56 * MIB
        ),
    )(partials, bias[:, None, :])


def shards(ny, features, weights, biases, dest_dev, dest_local):
    owners = lax.axis_size("rows")
    rank = lax.axis_index("rows")
    owned = features.shape[0]
    position = dest_dev[0] * owned + dest_local[0]
    position = lax.dynamic_slice_in_dim(position, rank * owned, owned, 0).reshape(-1)
    partials = local_partials(position, features, weights[0], owners, owned)
    return scatter_sum(partials, biases[0], owners // (2 * ny), ny)


def solution(mesh):
    ny = 4 // mesh.shape["groups"]
    in_specs = (
        P("rows", "groups", None),
        P(None, "rows", None, None, None),
        P(None, "rows", None),
        P(),
        P(),
    )
    return jax.shard_map(
        functools.partial(shards, ny), mesh=mesh, in_specs=in_specs,
        out_specs=P("rows", "groups", None), check_vma=False,
    )
```

```python
import functools

import jax
import jax.numpy as jnp
from jax import lax
from jax.experimental import pallas as pl
from jax.experimental.pallas import tpu as pltpu
from jax.sharding import PartitionSpec as P

MIB = 1024 * 1024


def partial_kernel(pos_ref, feat_ref, weight_ref, out_ref, acc, sem):
    step = pl.program_id(0)
    per_step, degree = weight_ref.shape[:2]
    owners, owned = acc.shape[:2]

    @pl.when(step == 0)
    def _():
        @pl.loop(0, owners)
        def _(o):
            @pl.loop(0, owned)
            def _(b):
                acc[o, b] = jnp.zeros(acc.shape[2:], acc.dtype)

    @pl.loop(0, per_step)
    def _(i):
        block = feat_ref[i]
        products = [
            jnp.dot(block, weight_ref[i, k], preferred_element_type=jnp.float32)
            for k in range(degree)
        ]
        base = (step * per_step + i) * degree
        for k in range(degree):
            position = pos_ref[base + k]
            acc[position // owned, position % owned] += products[k]

    @pl.when(step == pl.num_programs(0) - 1)
    def _():
        copy = pltpu.make_async_copy(acc, out_ref, sem)
        copy.start()
        copy.wait()


def local_partials(position, features, weights, owners, owned):
    count, samples, width = features.shape
    degree = weights.shape[1]
    per_step = min(4, count)
    return pl.pallas_call(
        partial_kernel,
        out_shape=jax.ShapeDtypeStruct((owners, owned, samples, width), jnp.float32),
        grid_spec=pltpu.PrefetchScalarGridSpec(
            num_scalar_prefetch=1,
            grid=(count // per_step,),
            in_specs=[
                pl.BlockSpec((per_step, samples, width), lambda s, pos: (s, 0, 0)),
                pl.BlockSpec((per_step, degree, width, width), lambda s, pos: (s, 0, 0, 0)),
            ],
            out_specs=pl.BlockSpec(memory_space=pl.ANY),
            scratch_shapes=[
                pltpu.VMEM((owners, owned, samples, width), jnp.float32),
                pltpu.SemaphoreType.DMA,
            ],
        ),
        compiler_params=pltpu.CompilerParams(
            dimension_semantics=("arbitrary",), vmem_limit_bytes=48 * MIB
        ),
    )(position, features, weights)


def farthest_first(z, nz):
    near = jnp.minimum(z, nz - 1 - z)
    far = nz - 1 - near
    sign = jnp.where(2 * z < nz, 1, -1)
    places = []
    for t in range(nz):
        u = t - (far - near)
        alone = z + sign * (far - t)
        paired = jnp.where(u % 2 == 0, z + sign * (near - u // 2), z - sign * (near - u // 2))
        places.append(jnp.where(u < 0, alone, paired))
    return places


def scatter_kernel(nz, ny, lead, p_ref, bias_ref, out_ref, held, own, from_y, from_low, from_high,
                   lead_y, lead_low, lead_high,
                   own_sem, c_send, c_recv, y_send, y_recv, up_send, up_recv, down_send, down_recv,
                   ly_send, ly_recv, lup_send, lup_recv, ldown_send, ldown_recv):
    rank = lax.axis_index("rows")
    c = rank % 2
    y = (rank // 2) % ny
    z = rank // (2 * ny)
    owned = out_ref.shape[0]

    def row(z_at, y_at, c_at):
        return (z_at * ny + y_at) * 2 + c_at

    def remote(src, dst, send, recv, target):
        return pltpu.make_async_remote_copy(
            src_ref=src, dst_ref=dst, send_sem=send, recv_sem=recv,
            device_id={"rows": target}, device_id_type=pl.DeviceIdType.MESH,
        )

    sibling = row(z, y, 1 - c)
    peer = row(z, ny - 1 - y, c)
    above = row(z + 1, y, c)
    below = row(z - 1, y, c)
    has_above, has_below = z < nz - 1, z > 0

    barrier = pltpu.get_barrier_semaphore()

    def greet(target):
        pl.semaphore_signal(
            barrier, inc=1, device_id={"rows": target}, device_id_type=pl.DeviceIdType.MESH
        )

    greet(sibling)
    if ny > 1:
        greet(peer)
    pl.when(has_above)(lambda: greet(above))
    pl.when(has_below)(lambda: greet(below))
    pl.semaphore_wait(barrier, ny + jnp.where(has_above, 1, 0) + jnp.where(has_below, 1, 0))

    def add(dst, src, start=0):
        @pl.loop(0, src.shape[0])
        def _(b):
            dst[b + start] += src[b]

    rest = pl.ds(lead, owned - lead)
    first = pl.ds(0, max(lead, 1))

    order = farthest_first(z, nz)

    def y_of(h):
        return y if h == ny - 1 else ny - 1 - y

    pieces = [(h, place) for place in order for h in range(ny)]

    def to_sibling(h, place):
        return remote(p_ref.at[row(place, y_of(h), 1 - c)], held.at[h, place],
                      c_send.at[h, place], c_recv.at[h, place], sibling)

    def load(n):
        h, place = pieces[n]
        return pltpu.make_async_copy(
            p_ref.at[row(place, y_of(h), c)], own.at[n % 2], own_sem.at[n % 2]
        )

    def to_peer(place):
        return remote(held.at[0, place, rest], from_y.at[place], y_send.at[place], y_recv.at[place], peer)

    def to_above(place):
        return remote(held.at[ny - 1, place, rest], from_low.at[place - 1],
                      up_send.at[place - 1], up_recv.at[place - 1], above)

    def to_below(place):
        return remote(held.at[ny - 1, place, rest], from_high.at[place],
                      down_send.at[place], down_recv.at[place], below)

    def lead_above(place):
        return remote(held.at[:, place, first], lead_low.at[place - 1],
                      lup_send.at[place - 1], lup_recv.at[place - 1], above)

    def lead_below(place):
        return remote(held.at[:, place, first], lead_high.at[place],
                      ldown_send.at[place], ldown_recv.at[place], below)

    def lead_peer():
        return remote(held.at[0, z, first], lead_y, ly_send, ly_recv, peer)

    def add_lead(place, src):
        for h in range(ny):
            add(held.at[h, place], src.at[h])

    load(0).start()
    for h, place in pieces:
        to_sibling(h, place).start()
    for n, (h, place) in enumerate(pieces):
        if n + 1 < len(pieces):
            load(n + 1).start()
        load(n).wait()
        to_sibling(h, place).wait_recv()
        add(held.at[h, place], own.at[n % 2])
        if h < ny - 1:
            to_peer(place).start()
        elif lead:
            pl.when((place > z) & (z == 0))(lambda: lead_above(place).start())
            pl.when((place < z) & (z == nz - 1))(lambda: lead_below(place).start())

    if lead:
        for place in order[:-1]:
            @pl.when((place > z) & has_below)
            def _():
                lead_above(place).wait_recv()
                add_lead(place, lead_low.at[place - 1])
                lead_above(place).start()

            @pl.when((place < z) & has_above)
            def _():
                lead_below(place).wait_recv()
                add_lead(place, lead_high.at[place])
                lead_below(place).start()

    for t, place in enumerate(order[:-1]):
        if ny > 1:
            to_peer(place).wait_recv()
            add(held.at[ny - 1, place], from_y.at[place], lead)

        @pl.when(place > z)
        def _():
            @pl.when(has_below)
            def _():
                to_above(place).wait_recv()
                add(held.at[ny - 1, place], from_low.at[place - 1], lead)
            to_above(place).start()

        @pl.when(place < z)
        def _():
            @pl.when(has_above)
            def _():
                to_below(place).wait_recv()
                add(held.at[ny - 1, place], from_high.at[place], lead)
            to_below(place).start()

        if lead and t == 1:
            @pl.when(has_below)
            def _():
                lead_above(z).wait_recv()
                add_lead(z, lead_low.at[z - 1])

            @pl.when(has_above)
            def _():
                lead_below(z).wait_recv()
                add_lead(z, lead_high.at[z])
            lead_peer().start()

    if ny > 1:
        to_peer(z).wait_recv()
        add(held.at[ny - 1, z], from_y.at[z], lead)
    if lead:
        lead_peer().wait_recv()
        add(held.at[ny - 1, z], lead_y)

    @pl.when(has_below)
    def _():
        to_above(z).wait_recv()
        add(held.at[ny - 1, z], from_low.at[z - 1], lead)

    @pl.when(has_above)
    def _():
        to_below(z).wait_recv()
        add(held.at[ny - 1, z], from_high.at[z], lead)

    @pl.loop(0, owned)
    def _(b):
        total = held[ny - 1, z, b] + bias_ref[b]
        out_ref[b] = jnp.maximum(total, 0.0).astype(out_ref.dtype)

    for h, place in pieces:
        to_sibling(h, place).wait_send()
    for place in order:
        if ny > 1:
            to_peer(place).wait_send()
        pl.when(place > z)(lambda place=place: to_above(place).wait_send())
        pl.when(place < z)(lambda place=place: to_below(place).wait_send())
        if lead:
            pl.when(place > z)(lambda place=place: lead_above(place).wait_send())
            pl.when(place < z)(lambda place=place: lead_below(place).wait_send())
    if lead:
        lead_peer().wait_send()


def scatter_sum(partials, bias, nz, ny):
    owners, owned, samples, width = partials.shape
    chunk = (owned, samples, width)
    lead = owned * 5 // 32 if ny > 1 and nz > 2 else 0
    rest = (owned - lead,) + chunk[1:]
    first = (max(lead, 1),) + chunk[1:]
    dma = pltpu.SemaphoreType.DMA
    vmem = pl.BlockSpec(memory_space=pltpu.VMEM)
    return pl.pallas_call(
        functools.partial(scatter_kernel, nz, ny, lead),
        out_shape=jax.ShapeDtypeStruct(chunk, jnp.bfloat16),
        in_specs=[pl.BlockSpec(memory_space=pl.ANY), vmem],
        out_specs=vmem,
        scratch_shapes=[
            pltpu.VMEM((ny, nz) + chunk, jnp.float32),
            pltpu.VMEM((2,) + chunk, jnp.float32),
            pltpu.VMEM((nz if ny > 1 else 1,) + rest, jnp.float32),
            pltpu.VMEM((nz - 1,) + rest, jnp.float32),
            pltpu.VMEM((nz - 1,) + rest, jnp.float32),
            pltpu.VMEM(first, jnp.float32),
            pltpu.VMEM((nz - 1, ny) + first if lead else (1, 1) + first, jnp.float32),
            pltpu.VMEM((nz - 1, ny) + first if lead else (1, 1) + first, jnp.float32),
            dma((2,)),
            dma((ny, nz)), dma((ny, nz)),
            dma((nz,)), dma((nz,)),
            dma((nz,)), dma((nz,)),
            dma((nz,)), dma((nz,)),
            dma, dma,
            dma((nz,)), dma((nz,)),
            dma((nz,)), dma((nz,)),
        ],
        compiler_params=pltpu.CompilerParams(
            collective_id=0, has_side_effects=True, vmem_limit_bytes=56 * MIB
        ),
    )(partials, bias[:, None, :])


def shards(ny, features, weights, biases, dest_dev, dest_local):
    owners = lax.axis_size("rows")
    rank = lax.axis_index("rows")
    owned = features.shape[0]
    position = dest_dev[0] * owned + dest_local[0]
    position = lax.dynamic_slice_in_dim(position, rank * owned, owned, 0).reshape(-1)
    partials = local_partials(position, features, weights[0], owners, owned)
    return scatter_sum(partials, biases[0], owners // (2 * ny), ny)


def solution(mesh):
    ny = 4 // mesh.shape["groups"]
    in_specs = (
        P("rows", "groups", None),
        P(None, "rows", None, None, None),
        P(None, "rows", None),
        P(),
        P(),
    )
    return jax.shard_map(
        functools.partial(shards, ny), mesh=mesh, in_specs=in_specs,
        out_specs=P("rows", "groups", None), check_vma=False,
    )
```

```python
import functools

import jax
import jax.numpy as jnp
from jax import lax
from jax.experimental import pallas as pl
from jax.experimental.pallas import tpu as pltpu
from jax.sharding import PartitionSpec as P

MIB = 1024 * 1024


def chunk_tables(dests, locals_, owners):
    owned, degree = dests.shape
    own = jnp.arange(owned, dtype=jnp.int32)
    named = dests[None] == jnp.arange(owners, dtype=jnp.int32)[:, None, None]
    entry = jnp.max(jnp.where(named, jnp.arange(degree, dtype=jnp.int32), 0), axis=2)
    entry = entry + own * degree
    block = jnp.max(jnp.where(named, locals_[None], -1), axis=2)
    same = (block[:, :, None] == block[:, None, :]) & (block[:, None, :] >= 0)
    earlier = same & (own[None, None, :] < own[None, :, None])
    before = jnp.max(jnp.where(earlier, own, -1), axis=2)
    last = jnp.max(jnp.where(block[:, None, :] == own[None, :, None], own, -1), axis=2)
    before = jnp.where(before < 0, owned, before)
    last = jnp.where(last < 0, owned, last)
    return jnp.stack([entry, before, last])


def farthest_first(z, nz):
    near = jnp.minimum(z, nz - 1 - z)
    far = nz - 1 - near
    sign = jnp.where(2 * z < nz, 1, -1)
    places = []
    for t in range(nz):
        u = t - (far - near)
        alone = z + sign * (far - t)
        paired = jnp.where(u % 2 == 0, z + sign * (near - u // 2), z - sign * (near - u // 2))
        places.append(jnp.where(u < 0, alone, paired))
    return places


def scatter_kernel(nz, ny, lead, table_ref, feat_ref, weight_hbm, bias_ref, out_ref,
                   weight_ref, held, sums, staged, from_y, from_low, from_high,
                   lead_y, lead_low, lead_high,
                   weight_sem, c_send, c_recv, y_send, y_recv, up_send, up_recv, down_send, down_recv,
                   ly_send, ly_recv, lup_send, lup_recv, ldown_send, ldown_recv):
    rank = lax.axis_index("rows")
    c = rank % 2
    y = (rank // 2) % ny
    z = rank // (2 * ny)
    owned = out_ref.shape[0]

    def row(z_at, y_at, c_at):
        return (z_at * ny + y_at) * 2 + c_at

    def remote(src, dst, send, recv, target):
        return pltpu.make_async_remote_copy(
            src_ref=src, dst_ref=dst, send_sem=send, recv_sem=recv,
            device_id={"rows": target}, device_id_type=pl.DeviceIdType.MESH,
        )

    sibling = row(z, y, 1 - c)
    peer = row(z, ny - 1 - y, c)
    above = row(z + 1, y, c)
    below = row(z - 1, y, c)
    has_above, has_below = z < nz - 1, z > 0

    load_weights = pltpu.make_async_copy(weight_hbm, weight_ref, weight_sem)
    load_weights.start()
    barrier = pltpu.get_barrier_semaphore()

    def greet(target):
        pl.semaphore_signal(
            barrier, inc=1, device_id={"rows": target}, device_id_type=pl.DeviceIdType.MESH
        )

    greet(sibling)
    if ny > 1:
        greet(peer)
    pl.when(has_above)(lambda: greet(above))
    pl.when(has_below)(lambda: greet(below))
    pl.semaphore_wait(barrier, ny + jnp.where(has_above, 1, 0) + jnp.where(has_below, 1, 0))

    def add(dst, src, start=0):
        @pl.loop(0, src.shape[0])
        def _(b):
            dst[b + start] += src[b]

    rest = pl.ds(lead, owned - lead)
    first = pl.ds(0, max(lead, 1))

    order = farthest_first(z, nz)

    def y_of(h):
        return y if h == ny - 1 else ny - 1 - y

    pieces = [(h, place) for place in order for h in range(ny)]

    def to_sibling(n):
        h, place = pieces[n]
        return remote(staged.at[n % 2], held.at[h, place],
                      c_send.at[h, place], c_recv.at[h, place], sibling)

    def add_products(owner):
        @pl.loop(0, owned, unroll=min(8, owned))
        def _(i):
            product = jnp.dot(
                feat_ref[i], weight_ref[table_ref[0, owner, i]], preferred_element_type=jnp.float32
            )
            sums[i] = product + sums[table_ref[1, owner, i]]

    def to_peer(place):
        return remote(held.at[0, place, rest], from_y.at[place], y_send.at[place], y_recv.at[place], peer)

    def to_above(place):
        return remote(held.at[ny - 1, place, rest], from_low.at[place - 1],
                      up_send.at[place - 1], up_recv.at[place - 1], above)

    def to_below(place):
        return remote(held.at[ny - 1, place, rest], from_high.at[place],
                      down_send.at[place], down_recv.at[place], below)

    def lead_above(place):
        return remote(held.at[:, place, first], lead_low.at[place - 1],
                      lup_send.at[place - 1], lup_recv.at[place - 1], above)

    def lead_below(place):
        return remote(held.at[:, place, first], lead_high.at[place],
                      ldown_send.at[place], ldown_recv.at[place], below)

    def lead_peer():
        return remote(held.at[0, z, first], lead_y, ly_send, ly_recv, peer)

    def add_lead(place, src):
        for h in range(ny):
            add(held.at[h, place], src.at[h])

    sums[owned] = jnp.zeros(sums.shape[1:], sums.dtype)
    load_weights.wait()
    for n, (h, place) in enumerate(pieces):
        theirs, mine = row(place, y_of(h), 1 - c), row(place, y_of(h), c)
        add_products(theirs)
        if n >= 2:
            to_sibling(n - 2).wait_send()

        @pl.loop(0, owned)
        def _(b):
            staged[n % 2, b] = sums[table_ref[2, theirs, b]]

        to_sibling(n).start()
        add_products(mine)
        to_sibling(n).wait_recv()

        @pl.loop(0, owned)
        def _(b):
            held[h, place, b] += sums[table_ref[2, mine, b]]

        if h < ny - 1:
            to_peer(place).start()
        elif lead:
            pl.when((place > z) & (z == 0))(lambda: lead_above(place).start())
            pl.when((place < z) & (z == nz - 1))(lambda: lead_below(place).start())

    if lead:
        for place in order[:-1]:
            @pl.when((place > z) & has_below)
            def _():
                lead_above(place).wait_recv()
                add_lead(place, lead_low.at[place - 1])
                lead_above(place).start()

            @pl.when((place < z) & has_above)
            def _():
                lead_below(place).wait_recv()
                add_lead(place, lead_high.at[place])
                lead_below(place).start()

    for t, place in enumerate(order[:-1]):
        if ny > 1:
            to_peer(place).wait_recv()
            add(held.at[ny - 1, place], from_y.at[place], lead)

        @pl.when(place > z)
        def _():
            @pl.when(has_below)
            def _():
                to_above(place).wait_recv()
                add(held.at[ny - 1, place], from_low.at[place - 1], lead)
            to_above(place).start()

        @pl.when(place < z)
        def _():
            @pl.when(has_above)
            def _():
                to_below(place).wait_recv()
                add(held.at[ny - 1, place], from_high.at[place], lead)
            to_below(place).start()

        if lead and t == 1:
            @pl.when(has_below)
            def _():
                lead_above(z).wait_recv()
                add_lead(z, lead_low.at[z - 1])

            @pl.when(has_above)
            def _():
                lead_below(z).wait_recv()
                add_lead(z, lead_high.at[z])
            lead_peer().start()

    if ny > 1:
        to_peer(z).wait_recv()
        add(held.at[ny - 1, z], from_y.at[z], lead)
    if lead:
        lead_peer().wait_recv()
        add(held.at[ny - 1, z], lead_y)

    @pl.when(has_below)
    def _():
        to_above(z).wait_recv()
        add(held.at[ny - 1, z], from_low.at[z - 1], lead)

    @pl.when(has_above)
    def _():
        to_below(z).wait_recv()
        add(held.at[ny - 1, z], from_high.at[z], lead)

    @pl.loop(0, owned)
    def _(b):
        total = held[ny - 1, z, b] + bias_ref[b]
        out_ref[b] = jnp.maximum(total, 0.0).astype(out_ref.dtype)

    for n in range(max(0, len(pieces) - 2), len(pieces)):
        to_sibling(n).wait_send()
    for place in order:
        if ny > 1:
            to_peer(place).wait_send()
        pl.when(place > z)(lambda place=place: to_above(place).wait_send())
        pl.when(place < z)(lambda place=place: to_below(place).wait_send())
        if lead:
            pl.when(place > z)(lambda place=place: lead_above(place).wait_send())
            pl.when(place < z)(lambda place=place: lead_below(place).wait_send())
    if lead:
        lead_peer().wait_send()


def scatter_sum(tables, features, weights, bias, nz, ny):
    owned, samples, width = features.shape
    chunk = (owned, samples, width)
    lead = owned * 5 // 32 if ny > 1 and nz > 2 else 0
    rest = (owned - lead,) + chunk[1:]
    first = (max(lead, 1),) + chunk[1:]
    dma = pltpu.SemaphoreType.DMA
    vmem = pl.BlockSpec(memory_space=pltpu.VMEM)
    return pl.pallas_call(
        functools.partial(scatter_kernel, nz, ny, lead),
        out_shape=jax.ShapeDtypeStruct(chunk, jnp.bfloat16),
        in_specs=[pl.BlockSpec(memory_space=pltpu.SMEM), vmem, pl.BlockSpec(memory_space=pl.ANY), vmem],
        out_specs=vmem,
        scratch_shapes=[
            pltpu.VMEM(weights.shape, weights.dtype),
            pltpu.VMEM((ny, nz) + chunk, jnp.float32),
            pltpu.VMEM((owned + 1,) + chunk[1:], jnp.float32),
            pltpu.VMEM((2,) + chunk, jnp.float32),
            pltpu.VMEM((nz if ny > 1 else 1,) + rest, jnp.float32),
            pltpu.VMEM((nz - 1,) + rest, jnp.float32),
            pltpu.VMEM((nz - 1,) + rest, jnp.float32),
            pltpu.VMEM(first, jnp.float32),
            pltpu.VMEM((nz - 1, ny) + first if lead else (1, 1) + first, jnp.float32),
            pltpu.VMEM((nz - 1, ny) + first if lead else (1, 1) + first, jnp.float32),
            dma,
            dma((ny, nz)), dma((ny, nz)),
            dma((nz,)), dma((nz,)),
            dma((nz,)), dma((nz,)),
            dma((nz,)), dma((nz,)),
            dma, dma,
            dma((nz,)), dma((nz,)),
            dma((nz,)), dma((nz,)),
        ],
        compiler_params=pltpu.CompilerParams(
            collective_id=0, has_side_effects=True, vmem_limit_bytes=60 * MIB
        ),
    )(tables, features, weights, bias[:, None, :])


def shards(ny, features, weights, biases, dest_dev, dest_local):
    owners = lax.axis_size("rows")
    rank = lax.axis_index("rows")
    owned = features.shape[0]
    dests, locals_ = (
        lax.dynamic_slice_in_dim(table[0], rank * owned, owned, 0) for table in (dest_dev, dest_local)
    )
    tables = chunk_tables(dests, locals_, owners)
    blocks = weights.reshape((-1,) + weights.shape[3:])
    return scatter_sum(tables, features, blocks, biases[0], owners // (2 * ny), ny)


def solution(mesh):
    ny = 4 // mesh.shape["groups"]
    in_specs = (
        P("rows", "groups", None),
        P(None, "rows", None, None, None),
        P(None, "rows", None),
        P(),
        P(),
    )
    return jax.shard_map(
        functools.partial(shards, ny), mesh=mesh, in_specs=in_specs,
        out_specs=P("rows", "groups", None), check_vma=False,
    )
```

```python
import functools

import jax
import jax.numpy as jnp
from jax import lax
from jax.experimental import pallas as pl
from jax.experimental.pallas import tpu as pltpu
from jax.sharding import PartitionSpec as P

MIB = 1024 * 1024


def chunk_tables(dests, locals_, owners):
    owned, degree = dests.shape
    own = jnp.arange(owned, dtype=jnp.int32)
    named = dests[None] == jnp.arange(owners, dtype=jnp.int32)[:, None, None]
    entry = jnp.max(jnp.where(named, jnp.arange(degree, dtype=jnp.int32), 0), axis=2)
    entry = entry + own * degree
    block = jnp.max(jnp.where(named, locals_[None], -1), axis=2)
    same = (block[:, :, None] == block[:, None, :]) & (block[:, None, :] >= 0)
    earlier = same & (own[None, None, :] < own[None, :, None])
    before = jnp.max(jnp.where(earlier, own, -1), axis=2)
    last = jnp.max(jnp.where(block[:, None, :] == own[None, :, None], own, -1), axis=2)
    before = jnp.where(before < 0, owned, before)
    last = jnp.where(last < 0, owned, last)
    return jnp.stack([entry, before, last])


def farthest_first(z, nz):
    near = jnp.minimum(z, nz - 1 - z)
    far = nz - 1 - near
    sign = jnp.where(2 * z < nz, 1, -1)
    places = []
    for t in range(nz):
        u = t - (far - near)
        alone = z + sign * (far - t)
        paired = jnp.where(u % 2 == 0, z + sign * (near - u // 2), z - sign * (near - u // 2))
        places.append(jnp.where(u < 0, alone, paired))
    return places


def scatter_kernel(nz, ny, lead, parts, table_ref, feat_ref, weight_hbm, bias_ref, out_ref,
                   weight_ref, held, sums, staged, from_y, from_low, from_high,
                   lead_y, lead_low, lead_high,
                   weight_sem, c_send, c_recv, y_send, y_recv, up_send, up_recv, down_send, down_recv,
                   ly_send, ly_recv, lup_send, lup_recv, ldown_send, ldown_recv):
    rank = lax.axis_index("rows")
    c = rank % 2
    y = (rank // 2) % ny
    z = rank // (2 * ny)
    owned = out_ref.shape[0]

    def row(z_at, y_at, c_at):
        return (z_at * ny + y_at) * 2 + c_at

    def remote(src, dst, send, recv, target):
        return pltpu.make_async_remote_copy(
            src_ref=src, dst_ref=dst, send_sem=send, recv_sem=recv,
            device_id={"rows": target}, device_id_type=pl.DeviceIdType.MESH,
        )

    sibling = row(z, y, 1 - c)
    peer = row(z, ny - 1 - y, c)
    above = row(z + 1, y, c)
    below = row(z - 1, y, c)
    has_above, has_below = z < nz - 1, z > 0

    load_weights = pltpu.make_async_copy(weight_hbm, weight_ref, weight_sem)
    load_weights.start()
    barrier = pltpu.get_barrier_semaphore()

    def greet(target):
        pl.semaphore_signal(
            barrier, inc=1, device_id={"rows": target}, device_id_type=pl.DeviceIdType.MESH
        )

    greet(sibling)
    if ny > 1:
        greet(peer)
    pl.when(has_above)(lambda: greet(above))
    pl.when(has_below)(lambda: greet(below))
    pl.semaphore_wait(barrier, ny + jnp.where(has_above, 1, 0) + jnp.where(has_below, 1, 0))

    def add(dst, src, start=0):
        @pl.loop(0, src.shape[0])
        def _(b):
            dst[b + start] += src[b]

    size = (owned - lead) // parts
    starts = [lead + q * size for q in range(parts)]
    sections = [(start, size) for start in starts] + ([(0, lead)] if lead else [])
    first = pl.ds(0, max(lead, 1))

    order = farthest_first(z, nz)

    def y_of(h):
        return y if h == ny - 1 else ny - 1 - y

    pieces = [(h, place) for place in order for h in range(ny)]

    def to_sibling(n, q):
        h, place = pieces[n]
        blocks = pl.ds(*sections[q])
        return remote(staged.at[n % 2, blocks], held.at[h, place, blocks],
                      c_send.at[h, place, q], c_recv.at[h, place, q], sibling)

    def add_products(owner):
        @pl.loop(0, owned, unroll=min(8, owned))
        def _(i):
            product = jnp.dot(
                feat_ref[i], weight_ref[table_ref[0, owner, i]], preferred_element_type=jnp.float32
            )
            sums[i] = product + sums[table_ref[1, owner, i]]

    def went(q):
        return pl.ds(starts[q], size)

    def came(q):
        return pl.ds(q * size, size)

    def to_peer(place, q):
        return remote(held.at[0, place, went(q)], from_y.at[place, came(q)],
                      y_send.at[place, q], y_recv.at[place, q], peer)

    def to_above(place, q):
        return remote(held.at[ny - 1, place, went(q)], from_low.at[place - 1, came(q)],
                      up_send.at[place - 1, q], up_recv.at[place - 1, q], above)

    def to_below(place, q):
        return remote(held.at[ny - 1, place, went(q)], from_high.at[place, came(q)],
                      down_send.at[place, q], down_recv.at[place, q], below)

    def take_y(place, q):
        if ny > 1:
            to_peer(place, q).wait_recv()
            add(held.at[ny - 1, place], from_y.at[place, came(q)], starts[q])

    def take_low(place, q):
        to_above(place, q).wait_recv()
        add(held.at[ny - 1, place], from_low.at[place - 1, came(q)], starts[q])

    def take_high(place, q):
        to_below(place, q).wait_recv()
        add(held.at[ny - 1, place], from_high.at[place, came(q)], starts[q])

    def finish(start, count):
        @pl.loop(start, start + count)
        def _(b):
            total = held[ny - 1, z, b] + bias_ref[b]
            out_ref[b] = jnp.maximum(total, 0.0).astype(out_ref.dtype)

    def lead_above(place):
        return remote(held.at[:, place, first], lead_low.at[place - 1],
                      lup_send.at[place - 1], lup_recv.at[place - 1], above)

    def lead_below(place):
        return remote(held.at[:, place, first], lead_high.at[place],
                      ldown_send.at[place], ldown_recv.at[place], below)

    def lead_peer():
        return remote(held.at[0, z, first], lead_y, ly_send, ly_recv, peer)

    def add_lead(place, src):
        for h in range(ny):
            add(held.at[h, place], src.at[h])

    sums[owned] = jnp.zeros(sums.shape[1:], sums.dtype)
    load_weights.wait()
    for n, (h, place) in enumerate(pieces):
        theirs, mine = row(place, y_of(h), 1 - c), row(place, y_of(h), c)
        add_products(theirs)
        if n >= 2:
            for q in range(len(sections)):
                to_sibling(n - 2, q).wait_send()
        for q, (start, count) in enumerate(sections):
            @pl.loop(start, start + count)
            def _(b):
                staged[n % 2, b] = sums[table_ref[2, theirs, b]]

            to_sibling(n, q).start()
        add_products(mine)
        for q, (start, count) in enumerate(sections):
            to_sibling(n, q).wait_recv()

            @pl.loop(start, start + count)
            def _(b):
                held[h, place, b] += sums[table_ref[2, mine, b]]

            if h < ny - 1 and q < parts:
                to_peer(place, q).start()
        if h == ny - 1 and lead:
            pl.when((place > z) & (z == 0))(lambda: lead_above(place).start())
            pl.when((place < z) & (z == nz - 1))(lambda: lead_below(place).start())

    if lead:
        for place in order[:-1]:
            @pl.when((place > z) & has_below)
            def _():
                lead_above(place).wait_recv()
                add_lead(place, lead_low.at[place - 1])
                lead_above(place).start()

            @pl.when((place < z) & has_above)
            def _():
                lead_below(place).wait_recv()
                add_lead(place, lead_high.at[place])
                lead_below(place).start()

    for t, place in enumerate(order[:-1]):
        for q in range(parts):
            take_y(place, q)

            @pl.when(place > z)
            def _():
                pl.when(has_below)(lambda: take_low(place, q))
                to_above(place, q).start()

            @pl.when(place < z)
            def _():
                pl.when(has_above)(lambda: take_high(place, q))
                to_below(place, q).start()

        if lead and t == 1:
            @pl.when(has_below)
            def _():
                lead_above(z).wait_recv()
                add_lead(z, lead_low.at[z - 1])

            @pl.when(has_above)
            def _():
                lead_below(z).wait_recv()
                add_lead(z, lead_high.at[z])
            lead_peer().start()

    for q in range(parts):
        take_y(z, q)
        pl.when(has_below)(lambda: take_low(z, q))
        pl.when(has_above)(lambda: take_high(z, q))
        finish(starts[q], size)
    if lead:
        lead_peer().wait_recv()
        add(held.at[ny - 1, z], lead_y)
        finish(0, lead)

    for n in range(max(0, len(pieces) - 2), len(pieces)):
        for q in range(len(sections)):
            to_sibling(n, q).wait_send()
    for place in order:
        for q in range(parts):
            if ny > 1:
                to_peer(place, q).wait_send()
            pl.when(place > z)(lambda: to_above(place, q).wait_send())
            pl.when(place < z)(lambda: to_below(place, q).wait_send())
        if lead:
            pl.when(place > z)(lambda: lead_above(place).wait_send())
            pl.when(place < z)(lambda: lead_below(place).wait_send())
    if lead:
        lead_peer().wait_send()


def scatter_sum(tables, features, weights, bias, nz, ny):
    owned, samples, width = features.shape
    chunk = (owned, samples, width)
    lead = owned * 5 // 32 if ny > 1 and nz > 2 else 0
    parts = next((p for p in (3, 2) if ny > 1 and (owned - lead) % p == 0), 1)
    rest = (owned - lead,) + chunk[1:]
    first = (max(lead, 1),) + chunk[1:]
    dma = pltpu.SemaphoreType.DMA
    vmem = pl.BlockSpec(memory_space=pltpu.VMEM)
    return pl.pallas_call(
        functools.partial(scatter_kernel, nz, ny, lead, parts),
        out_shape=jax.ShapeDtypeStruct(chunk, jnp.bfloat16),
        in_specs=[pl.BlockSpec(memory_space=pltpu.SMEM), vmem, pl.BlockSpec(memory_space=pl.ANY), vmem],
        out_specs=vmem,
        scratch_shapes=[
            pltpu.VMEM(weights.shape, weights.dtype),
            pltpu.VMEM((ny, nz) + chunk, jnp.float32),
            pltpu.VMEM((owned + 1,) + chunk[1:], jnp.float32),
            pltpu.VMEM((2,) + chunk, jnp.float32),
            pltpu.VMEM((nz if ny > 1 else 1,) + rest, jnp.float32),
            pltpu.VMEM((nz - 1,) + rest, jnp.float32),
            pltpu.VMEM((nz - 1,) + rest, jnp.float32),
            pltpu.VMEM(first, jnp.float32),
            pltpu.VMEM((nz - 1, ny) + first if lead else (1, 1) + first, jnp.float32),
            pltpu.VMEM((nz - 1, ny) + first if lead else (1, 1) + first, jnp.float32),
            dma,
            dma((ny, nz, parts + 1)), dma((ny, nz, parts + 1)),
            dma((nz, parts)), dma((nz, parts)),
            dma((nz, parts)), dma((nz, parts)),
            dma((nz, parts)), dma((nz, parts)),
            dma, dma,
            dma((nz,)), dma((nz,)),
            dma((nz,)), dma((nz,)),
        ],
        compiler_params=pltpu.CompilerParams(
            collective_id=0, has_side_effects=True, vmem_limit_bytes=60 * MIB
        ),
    )(tables, features, weights, bias[:, None, :])


def shards(ny, features, weights, biases, dest_dev, dest_local):
    owners = lax.axis_size("rows")
    rank = lax.axis_index("rows")
    owned = features.shape[0]
    dests, locals_ = (
        lax.dynamic_slice_in_dim(table[0], rank * owned, owned, 0) for table in (dest_dev, dest_local)
    )
    tables = chunk_tables(dests, locals_, owners)
    blocks = weights.reshape((-1,) + weights.shape[3:])
    return scatter_sum(tables, features, blocks, biases[0], owners // (2 * ny), ny)


def solution(mesh):
    ny = 4 // mesh.shape["groups"]
    in_specs = (
        P("rows", "groups", None),
        P(None, "rows", None, None, None),
        P(None, "rows", None),
        P(),
        P(),
    )
    return jax.shard_map(
        functools.partial(shards, ny), mesh=mesh, in_specs=in_specs,
        out_specs=P("rows", "groups", None), check_vma=False,
    )
```
